512 devices in a mesh: dp: 4 (over x), row: 32 (over z, core), col: 4 (over y).
Axes of the slice: x: 4, y: 4, z: 16, core: 2. Of those that a mesh axis runs over, the one named last changes fastest.
Arguments:
- gate_grads: bfloat16 [4, 4096, 16384], P('dp', 'row', 'col'), may hold values from -1000 to 1000
- gate_rows: float32 [4096], P('row'), may hold values from 0.002 to 1
- gate_cols: float32 [16384], P('col'), may hold values from 0.002 to 1
- out_grads: bfloat16 [4, 16384, 4096], P('dp', 'row', 'col'), may hold values from -1000 to 1000
- out_rows: float32 [16384], P('row'), may hold values from 0.002 to 1
- out_cols: float32 [4096], P('col'), may hold values from 0.002 to 1
Outputs:
- gate_update: bfloat16 [4096, 16384], P('row', 'col')
- gate_rows_new: float32 [4096], P('row')
- gate_cols_new: float32 [16384], P('col')
- out_update: bfloat16 [16384, 4096], P('row', 'col')
- out_rows_new: float32 [16384], P('row')
- out_cols_new: float32 [4096], P('col')
The draws below stay inside these ranges and needn't reach their ends.
All inputs are finite; a program needn't handle non-finite values.
Results may differ from the reference program's by a relative error of at most 0.015.
Values may be sent and summed in bfloat16 or wider, within the bound.
A program may use at most 64 MiB of HBM per device.

```python
import math
import jax
import jax.numpy as jnp
from jax import lax

D = 4096
FF = 16384
REPLICAS = 4


def grad_scale(key, n_rows, n_cols, rise, spread):
    key_rows, key_cols = jax.random.split(key, 2)
    row_scale = jnp.exp(jax.random.uniform(key_rows, (n_rows,), jnp.float32, 0.0, math.log(spread)))
    col_scale = jnp.exp(jax.random.uniform(key_cols, (n_cols,), jnp.float32, 0.0, math.log(spread)))
    row_pos = jnp.arange(n_rows, dtype=jnp.float32) / n_rows
    col_pos = jnp.arange(n_cols, dtype=jnp.float32) / n_cols
    row_scale = row_scale * rise ** row_pos
    col_scale = col_scale * rise ** col_pos
    shape = 3.0 ** (row_pos[:, None] * col_pos[None, :])
    return 0.005 * row_scale[:, None] * col_scale[None, :] * shape


def draw_gate_grads(key, part):
    key = jax.random.fold_in(key, 11)
    key_scale, key_noise = jax.random.split(key, 2)
    noise = jax.random.normal(key_noise, (REPLICAS, D, FF), jnp.float32)
    scale = grad_scale(key_scale, D, FF, 3.0, 10.0)
    return (noise * scale[None, :, :]).astype(jnp.bfloat16)


def draw_out_grads(key, part):
    key = jax.random.fold_in(key, 23)
    key_scale, key_noise = jax.random.split(key, 2)
    noise = jax.random.normal(key_noise, (REPLICAS, FF, D), jnp.float32)
    scale = grad_scale(key_scale, FF, D, 3.0, 10.0)
    return (noise * scale[None, :, :]).astype(jnp.bfloat16)


def level_of(own_key, extent, cuts, low, high):
    def one(axis_at, shards_of):
        draws = jax.random.uniform(jax.random.fold_in(jax.random.fold_in(own_key, 6), axis_at), (shards_of,), jnp.float32, low / len(cuts), high / len(cuts))
        return jnp.repeat(jnp.exp(draws), extent[axis_at] // shards_of).reshape((-1,) + (1,) * (len(extent) - axis_at - 1))

    loudness = one(*cuts[0])
    for cut in cuts[1:]:
        loudness = loudness * one(*cut)
    return loudness


def setup_inputs(seed: int = 0) -> dict:
    keys = jax.random.split(jax.random.key(seed), 7)
    return {
        "gate_grads": draw_gate_grads(jax.random.fold_in(keys[6], 71), 0),
        "gate_rows": jnp.clip(jnp.exp(math.log(1.0) - 6.214608 * jax.random.uniform(keys[1], (D,), jnp.float32) ** level_of(keys[1], (D,), ((0, 32),), -0.2, 0.2)), 0.002, 1.0),
        "gate_cols": jnp.clip(jnp.exp(math.log(1.0) - 6.214608 * jax.random.uniform(keys[2], (FF,), jnp.float32) ** level_of(keys[2], (FF,), ((0, 4),), -0.2, 0.2)), 0.002, 1.0),
        "out_grads": draw_out_grads(jax.random.fold_in(keys[6], 71), 0),
        "out_rows": jnp.clip(jnp.exp(math.log(1.0) - 6.214608 * jax.random.uniform(keys[4], (FF,), jnp.float32) ** level_of(keys[4], (FF,), ((0, 32),), -0.2, 0.2)), 0.002, 1.0),
        "out_cols": jnp.clip(jnp.exp(math.log(1.0) - 6.214608 * jax.random.uniform(keys[5], (D,), jnp.float32) ** level_of(keys[5], (D,), ((0, 4),), -0.2, 0.2)), 0.002, 1.0),
    }


beta_two = 0.8
tiny = 1e-30
clip_level = 1.0

def adafactor_one(grads, rows, cols):
    summed = grads[0].astype(jnp.float32)
    for replica in range(1, REPLICAS):
        summed = summed + grads[replica].astype(jnp.float32)
    squares = summed * summed + tiny
    rows_new = beta_two * rows + (1.0 - beta_two) * lax.optimization_barrier(jnp.mean(squares, axis=1))
    cols_new = beta_two * cols + (1.0 - beta_two) * lax.optimization_barrier(jnp.mean(squares, axis=0))
    row_mean = jnp.mean(rows_new)
    scaled = summed / jnp.sqrt(rows_new[:, None] * cols_new[None, :] / row_mean)
    root = jnp.sqrt(jnp.mean(scaled * scaled))
    update = (scaled / jnp.maximum(1.0, root / clip_level)).astype(jnp.bfloat16)
    return (update, rows_new, cols_new)

def reference(gate_grads, gate_rows, gate_cols, out_grads, out_rows, out_cols):
    gate_update, gate_rows_new, gate_cols_new = adafactor_one(gate_grads, gate_rows, gate_cols)
    out_update, out_rows_new, out_cols_new = adafactor_one(out_grads, out_rows, out_cols)
    return (gate_update, gate_rows_new, gate_cols_new, out_update, out_rows_new, out_cols_new)
```

```python
import functools

import jax
import jax.numpy as jnp
from jax import lax
from jax.experimental import pallas as pl
from jax.experimental.pallas import tpu as pltpu
from jax.sharding import PartitionSpec as P

D = 4096
FF = 16384
KEEP = 0.8
TINY = 1e-30
MESH = pl.DeviceIdType.MESH
F32 = jnp.float32
BF16 = jnp.bfloat16


class Mat:
    def __init__(self, rows, width, m, n, first_row):
        self.rows, self.width, self.m, self.n, self.first_row = rows, width, m, n, first_row
        self.chunk = width // 4
        self.half = rows // 2
        self.tiles = self.chunk // 128


GATE = Mat(128, 4096, D, FF, 0)
OUT = Mat(512, 1024, FF, D, 128)
MATS = (GATE, OUT)


def cols_of(mat, k):
    return pl.ds(pl.multiple_of(k * mat.chunk, 128), mat.chunk)


def half_of(mat, h):
    return pl.ds(h * mat.half, mat.half)


def rcopy(src, dst, send, recv, dev):
    return pltpu.make_async_remote_copy(
        src_ref=src, dst_ref=dst, send_sem=send, recv_sem=recv, device_id=dev, device_id_type=MESH
    )


def kernel(
    zs,
    gate_in, gate_rows, gate_cols, out_in, out_rows, out_cols,
    gate_up, gate_rows_new, gate_cols_new, out_up, out_rows_new, out_cols_new,
    own_g, own_o, tr_g, tr_o, st_g, st_o, fr_g, fr_o, full_g, full_o, res_g, res_o,
    sq_g, sq_o, lanes, rmat, rows_buf, q_mine, q_sib, q_z, w_mine, w_sib, w_z, e_buf, cf_g, cf_o,
    load_sem, store_sem, rs_send, rs_recv, ag_send, ag_recv,
    s1_send, s1_recv, core_send, core_recv, z_send, z_recv, s3_send, s3_recv,
):
    x, r, y = lax.axis_index("dp"), lax.axis_index("row"), lax.axis_index("col")
    z, core = r // 2, r % 2
    right, left, over = (x + 1) % 4, (x + 3) % 4, (x + 2) % 4
    dev = ((right, r, y), (left, r, y))
    sibling = (x, z * 2 + (1 - core), y)
    ins, own, tr, st, fr, full, res = (
        (gate_in, out_in), (own_g, own_o), (tr_g, tr_o), (st_g, st_o), (fr_g, fr_o), (full_g, full_o), (res_g, res_o),
    )

    loads = [
        pltpu.make_async_copy(ins[i].at[0], own[i], load_sem.at[i]) for i in range(2)
    ]
    for load in loads:
        load.start()

    xy_partners = [((x + i) % 4, (y + j) % 4) for i in range(4) for j in range(4) if i or j]
    z_partners = [(z + k) % zs for k in range(1, zs)]
    barrier = pltpu.get_barrier_semaphore()
    greet = (
        [(a, r, b) for a, b in xy_partners]
        + [(a, z * 2 + (1 - core), b) for a, b in xy_partners]
        + [sibling]
        + [(x, k * 2 + core, y) for k in z_partners]
    )
    for who in greet:
        pl.semaphore_signal(barrier, inc=1, device_id=who, device_id_type=MESH)
    q_mine[...] = jnp.zeros_like(q_mine)
    w_mine[...] = jnp.zeros_like(w_mine)
    for load in loads:
        load.wait()
    pl.semaphore_wait(barrier, len(greet))

    sends = []

    def go(copy):
        copy.start()
        sends.append(copy)

    def rs_transit(i, d):
        return rcopy(
            own[i].at[half_of(MATS[i], d), cols_of(MATS[i], over)], tr[i].at[d],
            rs_send.at[i, d, 0], rs_recv.at[i, d, 0], dev[d],
        )

    def rs_alone(i, d):
        to = (right, left)[d]
        return rcopy(
            own[i].at[half_of(MATS[i], 1 - d), cols_of(MATS[i], to)], fr[i].at[d, half_of(MATS[i], 1 - d)],
            rs_send.at[i, d, 1], rs_recv.at[i, d, 1], dev[d],
        )

    def rs_sum(i, d):
        return rcopy(
            st[i].at[d], fr[i].at[d, half_of(MATS[i], d)],
            rs_send.at[i, d, 2], rs_recv.at[i, d, 2], dev[d],
        )

    for make in (rs_transit, rs_alone):
        for i in range(2):
            for d in range(2):
                go(make(i, d))
    for i in range(2):
        mat = MATS[i]
        for d in range(2):
            to = (right, left)[d]
            rs_transit(i, d).wait_recv()
            step = 16384 // mat.chunk

            def add(n, _, i=i, d=d, to=to, mat=mat, step=step):
                rows = pl.ds(pl.multiple_of(n * step, 16), step)
                mine = own[i][pl.ds(pl.multiple_of(d * mat.half + n * step, 16), step), cols_of(mat, to)]
                st[i][d, rows, :] = (mine.astype(F32) + tr[i][d, rows, :].astype(F32)).astype(BF16)
                return 0

            lax.fori_loop(0, mat.half // step, add, 0)
            go(rs_sum(i, d))

    me_xy = x * 4 + y
    for i in range(2):
        mat = MATS[i]
        sq = (sq_g, sq_o)[i]
        for d in range(2):
            rs_alone(i, d).wait_recv()
            rs_sum(i, d).wait_recv()
        step = 16384 // mat.chunk

        def total(n, acc, i=i, mat=mat, sq=sq, step=step):
            rows = pl.ds(pl.multiple_of(n * step, 16), step)
            s = own[i][rows, cols_of(mat, x)].astype(F32) + fr[i][0, rows, :].astype(F32) + fr[i][1, rows, :].astype(F32)
            full[i][rows, cols_of(mat, x)] = s.astype(BF16)
            s = s * s
            sq[rows, :] = s
            by_lane = s[:, 0:128]
            for t in range(1, mat.tiles):
                by_lane = by_lane + s[:, t * 128 : (t + 1) * 128]
            lanes[pl.ds(pl.multiple_of(mat.first_row + n * step, 8), step), :] = by_lane
            for k in range(step // 8):
                acc = acc + s[k * 8 : (k + 1) * 8, :]
            return acc

        acc = lax.fori_loop(0, mat.rows // step, total, jnp.zeros((8, mat.chunk), F32))
        col = jnp.sum(acc, axis=0, keepdims=True)
        for h in range(2):
            for t in range(mat.tiles // 2):
                k = h * (mat.tiles // 2) + t
                at = t if i == 0 else 4
                q_mine[h, at : at + 1, :] = col[:, k * 128 : (k + 1) * 128]
    for b in range(5):
        block = lanes[b * 128 : (b + 1) * 128, :].T
        rows_buf[me_xy, b : b + 1, :] = jnp.sum(block, axis=0, keepdims=True)

    def s1(a, b, peer):
        return rcopy(
            rows_buf.at[me_xy if peer is None else peer, pl.ds(0, 5)], rows_buf.at[me_xy if peer is None else peer, pl.ds(0, 5)],
            s1_send.at[a * 4 + b], s1_recv.at[me_xy if peer is None else peer], (a, r, b),
        )

    for a, b in xy_partners:
        go(s1(a, b, None))

    def to_core(buf, got, j):
        return rcopy(buf.at[1 - core], got, core_send.at[j], core_recv.at[j], sibling)

    go(to_core(q_mine, q_sib, 0))

    def ag_own(i, d, p):
        h = d if p == 0 else 1 - d
        ref = full[i].at[half_of(MATS[i], h), cols_of(MATS[i], x)]
        return rcopy(ref, ref, ag_send.at[i, d, p], ag_recv.at[i, d, p], dev[d])

    def ag_landed(i, d, p):
        h = d if p != 1 else 1 - d
        k = over if p == 2 else (left, right)[d]
        ref = full[i].at[half_of(MATS[i], h), cols_of(MATS[i], k)]
        return rcopy(ref, ref, ag_send.at[i, d, p], ag_recv.at[i, d, p], dev[d])

    def ag_forward(i, d):
        ref = full[i].at[half_of(MATS[i], d), cols_of(MATS[i], (left, right)[d])]
        return rcopy(ref, ref, ag_send.at[i, d, 2], ag_recv.at[i, d, 2], dev[d])

    for p in range(2):
        for i in range(2):
            for d in range(2):
                go(ag_own(i, d, p))

    def to_z(buf, j, k, peer):
        slot = z if peer is None else peer
        return rcopy(
            buf.at[slot], buf.at[slot], z_send.at[j, k], z_recv.at[j, slot], (x, k * 2 + core, y)
        )

    to_core(q_mine, q_sib, 0).wait_recv()
    q_z[z] = q_mine[core] + q_sib[...]
    for k in z_partners:
        go(to_z(q_z, 0, k, None))

    for a, b in xy_partners:
        s1(a, b, a * 4 + b).wait_recv()
    row_sum = rows_buf[0, 0:5, :]
    for k in range(1, 16):
        row_sum = row_sum + rows_buf[k, 0:5, :]
    g_rows = KEEP * gate_rows[...] + (1.0 - KEEP) * (row_sum[0:1] * (1.0 / FF) + TINY)
    o_rows = KEEP * out_rows[...] + (1.0 - KEEP) * (row_sum[1:5] * (1.0 / D) + TINY)
    gate_rows_new[...] = g_rows
    out_rows_new[...] = o_rows
    for b in range(5):
        one = g_rows if b == 0 else o_rows[b - 1 : b]
        rmat[b * 128 : (b + 1) * 128, :] = jnp.broadcast_to(lax.rsqrt(one), (128, 128)).T

    for i in range(2):
        mat = MATS[i]
        sq = (sq_g, sq_o)[i]
        step = 16384 // mat.chunk

        def weigh(n, acc, mat=mat, sq=sq, step=step):
            f = rmat[pl.ds(pl.multiple_of(mat.first_row + n * step, 8), step), :]
            f = f * f
            out = []
            for t in range(mat.tiles):
                p = sq[pl.ds(pl.multiple_of(n * step, 8), step), t * 128 : (t + 1) * 128] * f
                a = acc[t]
                for k in range(step // 8):
                    a = a + p[k * 8 : (k + 1) * 8, :]
                out.append(a)
            return tuple(out)

        acc = lax.fori_loop(0, mat.rows // step, weigh, tuple(jnp.zeros((8, 128), F32) for _ in range(mat.tiles)))
        for h in range(2):
            for t in range(mat.tiles // 2):
                at = t if i == 0 else 4
                w_mine[h, at : at + 1, :] = jnp.sum(acc[h * (mat.tiles // 2) + t], axis=0, keepdims=True)
    for h in range(2):
        w_mine[h, 5:6, :] = g_rows
        w_mine[h, 6:7, :] = jnp.sum(o_rows, axis=0, keepdims=True)
    go(to_core(w_mine, w_sib, 1))
    to_core(w_mine, w_sib, 1).wait_recv()
    w_z[z] = w_mine[core] + w_sib[...]
    for k in z_partners:
        go(to_z(w_z, 1, k, None))

    for i in range(2):
        for d in range(2):
            ag_landed(i, d, 0).wait_recv()
            go(ag_forward(i, d))

    for k in z_partners:
        to_z(q_z, 0, k, k).wait_recv()
    q = q_z[0]
    for k in range(1, zs):
        q = q + q_z[k]
    old_g = gate_cols[pl.ds(pl.multiple_of(x * 8 + core * 4, 4), 4), :]
    old_o = out_cols[pl.ds(x * 2 + core, 1), :]
    c_g = KEEP * old_g + (1.0 - KEEP) * (q[0:4] * (1.0 / D) + TINY)
    c_o = KEEP * old_o + (1.0 - KEEP) * (q[4:5] * (1.0 / FF) + TINY)
    for k in z_partners:
        to_z(w_z, 1, k, k).wait_recv()
    w = w_z[0]
    for k in range(1, zs):
        w = w + w_z[k]
    me_e = (x * 4 + y) * 2 + core
    e_buf[me_e, 0:4, :] = c_g
    e_buf[me_e, 4:5, :] = c_o
    e_buf[me_e, 5:6, :] = jnp.sum(w[0:4] / c_g, axis=0, keepdims=True)
    e_buf[me_e, 6:7, :] = w[4:5] / c_o
    e_buf[me_e, 7:8, :] = jnp.zeros((1, 128), F32)

    def s3(a, b, h, peer):
        slot = me_e if peer is None else peer
        return rcopy(
            e_buf.at[slot], e_buf.at[slot], s3_send.at[(a * 4 + b) * 2 + h], s3_recv.at[slot], (a, z * 2 + h, b)
        )

    e_partners = [(x, y, 1 - core)] + [(a, b, h) for a, b in xy_partners for h in (core, 1 - core)]
    for a, b, h in e_partners:
        go(s3(a, b, h, None))

    row_total = (jnp.sum(w[5:6]), jnp.sum(w[6:7]))
    for i in range(2):
        for d in range(2):
            for p in (1, 2):
                ag_landed(i, d, p).wait_recv()
    for a, b, h in e_partners:
        s3(a, b, h, (a * 4 + b) * 2 + h).wait_recv()
    e = e_buf[0, 5:7, :]
    for k in range(1, 32):
        e = e + e_buf[k, 5:7, :]
    factors = []
    for i in range(2):
        mean = row_total[i] * (1.0 / MATS[i].m)
        energy = jnp.sum(e[i : i + 1])
        mean = jnp.full((1, 128), mean, F32)
        root = jnp.sqrt(mean * (energy * (1.0 / (D * FF))))
        factors.append(jnp.sqrt(mean) / jnp.maximum(1.0, root))
    for k in range(4):
        for h in range(2):
            slot = (k * 4 + y) * 2 + h
            gate_cols_new[8 * k + 4 * h : 8 * k + 4 * h + 4, :] = e_buf[slot, 0:4, :]
            out_cols_new[2 * k + h : 2 * k + h + 1, :] = e_buf[slot, 4:5, :]
    cf_g[...] = lax.rsqrt(gate_cols_new[...]) * factors[0]
    cf_o[...] = lax.rsqrt(out_cols_new[...]) * factors[1]

    stores = []
    for k in range(4):

        def scale(t, _, k=k):
            cols = pl.ds(pl.multiple_of((k * 8 + t) * 128, 128), 128)
            res_g[:, cols] = (full_g[:, cols].astype(F32) * rmat[0:128, :] * cf_g[pl.ds(k * 8 + t, 1), :]).astype(BF16)
            return 0

        lax.fori_loop(0, 8, scale, 0)
        part = res_g.at[:, pl.ds(k * 1024, 1024)]
        stores.append(pltpu.make_async_copy(part, gate_up.at[:, pl.ds(k * 1024, 1024)], store_sem.at[k]))
        stores[-1].start()
    for k in range(4):

        def scale(t, _, k=k):
            cols = pl.ds(pl.multiple_of(t * 128, 128), 128)
            rows = pl.ds(k * 128, 128)
            res_o[rows, cols] = (full_o[rows, cols].astype(F32) * rmat[(k + 1) * 128 : (k + 2) * 128, :] * cf_o[pl.ds(t, 1), :]).astype(BF16)
            return 0

        lax.fori_loop(0, 8, scale, 0)
        part = res_o.at[pl.ds(k * 128, 128)]
        stores.append(pltpu.make_async_copy(part, out_up.at[pl.ds(k * 128, 128)], store_sem.at[4 + k]))
        stores[-1].start()
    for copy in sends:
        copy.wait_send()
    for store in stores:
        store.wait()


def local(zs, gate_grads, gate_rows, gate_cols, out_grads, out_rows, out_cols):
    vmem, hbm = pl.BlockSpec(memory_space=pltpu.VMEM), pl.BlockSpec(memory_space=pl.ANY)
    dma, buf = pltpu.SemaphoreType.DMA, pltpu.VMEM
    tile = (8, 128)
    outs = pl.pallas_call(
        functools.partial(kernel, zs),
        out_shape=(
            jax.ShapeDtypeStruct((128, 4096), BF16),
            jax.ShapeDtypeStruct((1, 128), F32),
            jax.ShapeDtypeStruct((32, 128), F32),
            jax.ShapeDtypeStruct((512, 1024), BF16),
            jax.ShapeDtypeStruct((4, 128), F32),
            jax.ShapeDtypeStruct((8, 128), F32),
        ),
        in_specs=[hbm, vmem, vmem, hbm, vmem, vmem],
        out_specs=(hbm, vmem, vmem, hbm, vmem, vmem),
        scratch_shapes=[
            buf((128, 4096), BF16), buf((512, 1024), BF16),
            buf((2, 64, 1024), BF16), buf((2, 256, 256), BF16),
            buf((2, 64, 1024), BF16), buf((2, 256, 256), BF16),
            buf((2, 128, 1024), BF16), buf((2, 512, 256), BF16),
            buf((128, 4096), BF16), buf((512, 1024), BF16),
            buf((128, 4096), BF16), buf((512, 1024), BF16),
            buf((128, 1024), F32), buf((512, 256), F32),
            buf((640, 128), F32), buf((640, 128), F32),
            buf((16, *tile), F32),
            buf((2, *tile), F32), buf(tile, F32), buf((zs, *tile), F32),
            buf((2, *tile), F32), buf(tile, F32), buf((zs, *tile), F32),
            buf((32, *tile), F32), buf((32, 128), F32), buf(tile, F32),
            dma((2,)), dma((8,)), dma((2, 2, 3)), dma((2, 2, 3)), dma((2, 2, 3)), dma((2, 2, 3)),
            dma((16,)), dma((16,)), dma((2,)), dma((2,)), dma((2, zs)), dma((2, zs)), dma((32,)), dma((32,)),
        ],
        compiler_params=pltpu.CompilerParams(collective_id=0, has_side_effects=True, vmem_limit_bytes=48 << 20),
    )(
        gate_grads, gate_rows.reshape(1, 128), gate_cols.reshape(32, 128),
        out_grads, out_rows.reshape(4, 128), out_cols.reshape(8, 128),
    )
    gate_up, gate_r, gate_c, out_up, out_r, out_c = outs
    return gate_up, gate_r.reshape(128), gate_c.reshape(4096), out_up, out_r.reshape(512), out_c.reshape(1024)


def solution(mesh):
    in_specs = (P("dp", "row", "col"), P("row"), P("col"), P("dp", "row", "col"), P("row"), P("col"))
    out_specs = (P("row", "col"), P("row"), P("col"), P("row", "col"), P("row"), P("col"))
    return jax.shard_map(
        functools.partial(local, mesh.shape["row"] // 2), mesh=mesh, in_specs=in_specs, out_specs=out_specs, check_vma=False
    )
```

```python
import functools

import jax
import jax.numpy as jnp
from jax import lax
from jax.experimental import pallas as pl
from jax.experimental.pallas import tpu as pltpu
from jax.sharding import PartitionSpec as P

D = 4096
FF = 16384
KEEP = 0.8
TINY = 1e-30
MESH = pl.DeviceIdType.MESH
F32 = jnp.float32
BF16 = jnp.bfloat16


class Mat:
    def __init__(self, rows, width, m, n, first_row):
        self.rows, self.width, self.m, self.n, self.first_row = rows, width, m, n, first_row
        self.chunk = width // 4
        self.half = rows // 2
        self.tiles = self.chunk // 128


GATE = Mat(128, 4096, D, FF, 0)
OUT = Mat(512, 1024, FF, D, 128)
MATS = (GATE, OUT)


def cols_of(mat, k):
    return pl.ds(pl.multiple_of(k * mat.chunk, 128), mat.chunk)


def half_of(mat, h):
    return pl.ds(h * mat.half, mat.half)


def rcopy(src, dst, send, recv, dev):
    return pltpu.make_async_remote_copy(
        src_ref=src, dst_ref=dst, send_sem=send, recv_sem=recv, device_id=dev, device_id_type=MESH
    )


def kernel(
    zs,
    gate_in, gate_rows_in, gate_cols_in, out_in, out_rows_in, out_cols_in,
    full_g, full_o, rmat, cf_g, cf_o, gate_rows_new, gate_cols_new, out_rows_new, out_cols_new,
    gate_rows, gate_cols, out_rows, out_cols,
    own_g, own_o, tr_g, tr_o, st_g, st_o, fr_g, fr_o,
    sq_g, sq_o, lanes, rows_buf, q_mine, q_sib, q_z, w_mine, w_sib, w_z, e_buf,
    token, load_sem, rs_send, rs_recv, ag_send, ag_recv,
    s1_send, s1_recv, core_send, core_recv, z_send, z_recv, s3_send, s3_recv,
):
    x, r, y = lax.axis_index("dp"), lax.axis_index("row"), lax.axis_index("col")
    z, core = r // 2, r % 2
    right, left, over = (x + 1) % 4, (x + 3) % 4, (x + 2) % 4
    dev = ((right, r, y), (left, r, y))
    sibling = (x, z * 2 + (1 - core), y)
    own, tr, st, fr, full = (own_g, own_o), (tr_g, tr_o), (st_g, st_o), (fr_g, fr_o), (full_g, full_o)

    loads = [
        pltpu.make_async_copy(src, dst, load_sem.at[i])
        for i, (src, dst) in enumerate(
            (
                (gate_in.at[0], own_g), (out_in.at[0], own_o),
                (gate_rows_in, gate_rows), (gate_cols_in, gate_cols), (out_rows_in, out_rows), (out_cols_in, out_cols),
            )
        )
    ]
    for load in loads:
        load.start()

    xy_partners = [((x + i) % 4, (y + j) % 4) for i in range(4) for j in range(4) if i or j]
    z_partners = [(z + k) % zs for k in range(1, zs)]
    along_z = lambda k: (x, ((z + k + zs) % zs) * 2 + core, y)
    across_x, across_y = (over, r, y), (x, r, (y + 2) % 4)
    nearest = [dev[0], dev[1], (x, r, (y + 1) % 4), (x, r, (y + 3) % 4), along_z(1), along_z(-1), sibling]
    rounds = (nearest, [across_x, across_y, along_z(2), along_z(-2), sibling], [along_z(4), along_z(-4), across_x])

    def tell(k):
        for who in rounds[k]:
            pl.semaphore_signal(token.at[k], inc=1, device_id=who, device_id_type=MESH)

    def hear(k):
        pl.semaphore_wait(token.at[k], len(rounds[k]))

    barrier = pltpu.get_barrier_semaphore()
    for who in nearest:
        pl.semaphore_signal(barrier, inc=1, device_id=who, device_id_type=MESH)
    q_mine[...] = jnp.zeros_like(q_mine)
    w_mine[...] = jnp.zeros_like(w_mine)
    for load in loads:
        load.wait()
    pl.semaphore_wait(barrier, len(nearest))

    sends = []

    def go(copy):
        copy.start()
        sends.append(copy)

    def rs_transit(i, d):
        return rcopy(
            own[i].at[half_of(MATS[i], d), cols_of(MATS[i], over)], tr[i].at[d],
            rs_send.at[i, d, 0], rs_recv.at[i, d, 0], dev[d],
        )

    def rs_alone(i, d):
        to = (right, left)[d]
        return rcopy(
            own[i].at[half_of(MATS[i], 1 - d), cols_of(MATS[i], to)], fr[i].at[d, half_of(MATS[i], 1 - d)],
            rs_send.at[i, d, 1], rs_recv.at[i, d, 1], dev[d],
        )

    def rs_sum(i, d):
        return rcopy(
            st[i].at[d], fr[i].at[d, half_of(MATS[i], d)],
            rs_send.at[i, d, 2], rs_recv.at[i, d, 2], dev[d],
        )

    for make in (rs_transit, rs_alone):
        for i in range(2):
            for d in range(2):
                go(make(i, d))
    tell(0)
    for i in range(2):
        mat = MATS[i]
        for d in range(2):
            to = (right, left)[d]
            rs_transit(i, d).wait_recv()
            step = 16384 // mat.chunk

            def add(n, _, i=i, d=d, to=to, mat=mat, step=step):
                rows = pl.ds(pl.multiple_of(n * step, 16), step)
                mine = own[i][pl.ds(pl.multiple_of(d * mat.half + n * step, 16), step), cols_of(mat, to)]
                st[i][d, rows, :] = (mine.astype(F32) + tr[i][d, rows, :].astype(F32)).astype(BF16)
                return 0

            lax.fori_loop(0, mat.half // step, add, 0)
            go(rs_sum(i, d))
        hear(i)
        tell(i + 1)

    def ag_own(i, d, p):
        h = d if p == 0 else 1 - d
        ref = full[i].at[half_of(MATS[i], h), cols_of(MATS[i], x)]
        return rcopy(ref, ref, ag_send.at[i, d, p], ag_recv.at[i, d, p], dev[d])

    def ag_landed(i, d, p):
        h = d if p != 1 else 1 - d
        k = over if p == 2 else (left, right)[d]
        ref = full[i].at[half_of(MATS[i], h), cols_of(MATS[i], k)]
        return rcopy(ref, ref, ag_send.at[i, d, p], ag_recv.at[i, d, p], dev[d])

    def ag_forward(i, d):
        ref = full[i].at[half_of(MATS[i], d), cols_of(MATS[i], (left, right)[d])]
        return rcopy(ref, ref, ag_send.at[i, d, 2], ag_recv.at[i, d, 2], dev[d])

    me_xy = x * 4 + y
    for i in range(2):
        mat = MATS[i]
        sq = (sq_g, sq_o)[i]
        for d in range(2):
            rs_alone(i, d).wait_recv()
            rs_sum(i, d).wait_recv()
        step = 16384 // mat.chunk

        def total(n, acc, i=i, mat=mat, sq=sq, step=step):
            rows = pl.ds(pl.multiple_of(n * step, 16), step)
            s = own[i][rows, cols_of(mat, x)].astype(F32) + fr[i][0, rows, :].astype(F32) + fr[i][1, rows, :].astype(F32)
            full[i][rows, cols_of(mat, x)] = s.astype(BF16)
            s = s * s
            sq[rows, :] = s
            by_lane = s[:, 0:128]
            for t in range(1, mat.tiles):
                by_lane = by_lane + s[:, t * 128 : (t + 1) * 128]
            lanes[pl.ds(pl.multiple_of(mat.first_row + n * step, 8), step), :] = by_lane
            for k in range(step // 8):
                acc = acc + s[k * 8 : (k + 1) * 8, :]
            return acc

        acc = lax.fori_loop(0, mat.rows // step, total, jnp.zeros((8, mat.chunk), F32))
        col = jnp.sum(acc, axis=0, keepdims=True)
        for h in range(2):
            for t in range(mat.tiles // 2):
                k = h * (mat.tiles // 2) + t
                at = t if i == 0 else 4
                q_mine[h, at : at + 1, :] = col[:, k * 128 : (k + 1) * 128]
        if i == 0:
            for d in range(2):
                go(ag_own(i, d, 0))
    for b in range(5):
        block = lanes[b * 128 : (b + 1) * 128, :].T
        rows_buf[me_xy, b : b + 1, :] = jnp.sum(block, axis=0, keepdims=True)

    hear(2)
    def s1(a, b, peer):
        return rcopy(
            rows_buf.at[me_xy if peer is None else peer, pl.ds(0, 5)], rows_buf.at[me_xy if peer is None else peer, pl.ds(0, 5)],
            s1_send.at[a * 4 + b], s1_recv.at[me_xy if peer is None else peer], (a, r, b),
        )

    for a, b in xy_partners:
        go(s1(a, b, None))

    def to_core(buf, got, j):
        return rcopy(buf.at[1 - core], got, core_send.at[j], core_recv.at[j], sibling)

    go(to_core(q_mine, q_sib, 0))

    for i, p in ((1, 0), (0, 1), (1, 1)):
        for d in range(2):
            go(ag_own(i, d, p))

    def to_z(buf, j, k, peer):
        slot = z if peer is None else peer
        return rcopy(
            buf.at[slot], buf.at[slot], z_send.at[j, k], z_recv.at[j, slot], (x, k * 2 + core, y)
        )

    to_core(q_mine, q_sib, 0).wait_recv()
    q_z[z] = q_mine[core] + q_sib[...]
    for k in z_partners:
        go(to_z(q_z, 0, k, None))

    for a, b in xy_partners:
        s1(a, b, a * 4 + b).wait_recv()
    row_sum = rows_buf[0, 0:5, :]
    for k in range(1, 16):
        row_sum = row_sum + rows_buf[k, 0:5, :]
    g_rows = KEEP * gate_rows[...] + (1.0 - KEEP) * (row_sum[0:1] * (1.0 / FF) + TINY)
    o_rows = KEEP * out_rows[...] + (1.0 - KEEP) * (row_sum[1:5] * (1.0 / D) + TINY)
    gate_rows_new[...] = g_rows
    out_rows_new[...] = o_rows
    for b in range(5):
        one = g_rows if b == 0 else o_rows[b - 1 : b]
        rmat[b * 128 : (b + 1) * 128, :] = jnp.broadcast_to(lax.rsqrt(one), (128, 128)).T

    for i in range(2):
        mat = MATS[i]
        sq = (sq_g, sq_o)[i]
        step = 16384 // mat.chunk

        def weigh(n, acc, mat=mat, sq=sq, step=step):
            f = rmat[pl.ds(pl.multiple_of(mat.first_row + n * step, 8), step), :]
            f = f * f
            out = []
            for t in range(mat.tiles):
                p = sq[pl.ds(pl.multiple_of(n * step, 8), step), t * 128 : (t + 1) * 128] * f
                a = acc[t]
                for k in range(step // 8):
                    a = a + p[k * 8 : (k + 1) * 8, :]
                out.append(a)
            return tuple(out)

        acc = lax.fori_loop(0, mat.rows // step, weigh, tuple(jnp.zeros((8, 128), F32) for _ in range(mat.tiles)))
        for h in range(2):
            for t in range(mat.tiles // 2):
                at = t if i == 0 else 4
                w_mine[h, at : at + 1, :] = jnp.sum(acc[h * (mat.tiles // 2) + t], axis=0, keepdims=True)
    for h in range(2):
        w_mine[h, 5:6, :] = g_rows
        w_mine[h, 6:7, :] = jnp.sum(o_rows, axis=0, keepdims=True)
    go(to_core(w_mine, w_sib, 1))
    to_core(w_mine, w_sib, 1).wait_recv()
    w_z[z] = w_mine[core] + w_sib[...]
    for k in z_partners:
        go(to_z(w_z, 1, k, None))

    for i in range(2):
        for d in range(2):
            ag_landed(i, d, 0).wait_recv()
            go(ag_forward(i, d))

    for k in z_partners:
        to_z(q_z, 0, k, k).wait_recv()
    q = q_z[0]
    for k in range(1, zs):
        q = q + q_z[k]
    old_g = gate_cols[pl.ds(pl.multiple_of(x * 8 + core * 4, 4), 4), :]
    old_o = out_cols[pl.ds(x * 2 + core, 1), :]
    c_g = KEEP * old_g + (1.0 - KEEP) * (q[0:4] * (1.0 / D) + TINY)
    c_o = KEEP * old_o + (1.0 - KEEP) * (q[4:5] * (1.0 / FF) + TINY)
    for k in z_partners:
        to_z(w_z, 1, k, k).wait_recv()
    w = w_z[0]
    for k in range(1, zs):
        w = w + w_z[k]
    me_e = (x * 4 + y) * 2 + core
    e_buf[me_e, 0:4, :] = c_g
    e_buf[me_e, 4:5, :] = c_o
    e_buf[me_e, 5:6, :] = jnp.sum(w[0:4] / c_g, axis=0, keepdims=True)
    e_buf[me_e, 6:7, :] = w[4:5] / c_o
    e_buf[me_e, 7:8, :] = jnp.zeros((1, 128), F32)

    def s3(a, b, h, peer):
        slot = me_e if peer is None else peer
        return rcopy(
            e_buf.at[slot], e_buf.at[slot], s3_send.at[(a * 4 + b) * 2 + h], s3_recv.at[slot], (a, z * 2 + h, b)
        )

    e_partners = [(x, y, 1 - core)] + [(a, b, h) for a, b in xy_partners for h in (core, 1 - core)]
    for a, b, h in e_partners:
        go(s3(a, b, h, None))

    row_total = (jnp.sum(w[5:6]), jnp.sum(w[6:7]))
    for i in range(2):
        for d in range(2):
            for p in (1, 2):
                ag_landed(i, d, p).wait_recv()
    for a, b, h in e_partners:
        s3(a, b, h, (a * 4 + b) * 2 + h).wait_recv()
    e = e_buf[0, 5:7, :]
    for k in range(1, 32):
        e = e + e_buf[k, 5:7, :]
    factors = []
    for i in range(2):
        mean = row_total[i] * (1.0 / MATS[i].m)
        energy = jnp.sum(e[i : i + 1])
        mean = jnp.full((1, 128), mean, F32)
        root = jnp.sqrt(mean * (energy * (1.0 / (D * FF))))
        factors.append(jnp.sqrt(mean) / jnp.maximum(1.0, root))
    for k in range(4):
        for h in range(2):
            slot = (k * 4 + y) * 2 + h
            gate_cols_new[8 * k + 4 * h : 8 * k + 4 * h + 4, :] = e_buf[slot, 0:4, :]
            out_cols_new[2 * k + h : 2 * k + h + 1, :] = e_buf[slot, 4:5, :]
    cf_g[...] = lax.rsqrt(gate_cols_new[...]) * factors[0]
    cf_o[...] = lax.rsqrt(out_cols_new[...]) * factors[1]

    for copy in sends:
        copy.wait_send()


def finish(
    full_g, full_o, rmat, cf_g, cf_o, gate_r, gate_c, out_r, out_c,
    gate_up, gate_rows_new, gate_cols_new, out_up, out_rows_new, out_cols_new,
    res_g, res_o, store_sem,
):
    stores = []

    def store(src, dst):
        stores.append(pltpu.make_async_copy(src, dst, store_sem.at[len(stores)]))
        stores[-1].start()

    store(gate_r, gate_rows_new)
    store(gate_c, gate_cols_new)
    store(out_r, out_rows_new)
    store(out_c, out_cols_new)
    for k in range(4):

        def scale(t, _, k=k):
            cols = pl.ds(pl.multiple_of((k * 8 + t) * 128, 128), 128)
            res_g[:, cols] = (full_g[:, cols].astype(F32) * rmat[0:128, :] * cf_g[pl.ds(k * 8 + t, 1), :]).astype(BF16)
            return 0

        lax.fori_loop(0, 8, scale, 0)
        part = pl.ds(k * 1024, 1024)
        store(res_g.at[:, part], gate_up.at[:, part])
    for k in range(4):

        def scale(t, _, k=k):
            cols = pl.ds(pl.multiple_of(t * 128, 128), 128)
            rows = pl.ds(k * 128, 128)
            by_row = rmat[(k + 1) * 128 : (k + 2) * 128, :]
            res_o[rows, cols] = (full_o[rows, cols].astype(F32) * by_row * cf_o[pl.ds(t, 1), :]).astype(BF16)
            return 0

        lax.fori_loop(0, 8, scale, 0)
        part = pl.ds(k * 128, 128)
        store(res_o.at[part], out_up.at[part])
    for copy in stores:
        copy.wait()


def local(zs, gate_grads, gate_rows, gate_cols, out_grads, out_rows, out_cols):
    vmem, hbm = pl.BlockSpec(memory_space=pltpu.VMEM), pl.BlockSpec(memory_space=pltpu.HBM)
    dma, buf = pltpu.SemaphoreType.DMA, pltpu.VMEM
    tile = (8, 128)
    held = pl.pallas_call(
        functools.partial(kernel, zs),
        out_shape=(
            jax.ShapeDtypeStruct((128, 4096), BF16),
            jax.ShapeDtypeStruct((512, 1024), BF16),
            jax.ShapeDtypeStruct((640, 128), F32),
            jax.ShapeDtypeStruct((32, 128), F32),
            jax.ShapeDtypeStruct((8, 128), F32),
            jax.ShapeDtypeStruct((1, 128), F32),
            jax.ShapeDtypeStruct((32, 128), F32),
            jax.ShapeDtypeStruct((4, 128), F32),
            jax.ShapeDtypeStruct((8, 128), F32),
        ),
        in_specs=[hbm] * 6,
        out_specs=(vmem,) * 9,
        scratch_shapes=[
            buf((1, 128), F32), buf((32, 128), F32), buf((4, 128), F32), buf((8, 128), F32),
            buf((128, 4096), BF16), buf((512, 1024), BF16),
            buf((2, 64, 1024), BF16), buf((2, 256, 256), BF16),
            buf((2, 64, 1024), BF16), buf((2, 256, 256), BF16),
            buf((2, 128, 1024), BF16), buf((2, 512, 256), BF16),
            buf((128, 1024), F32), buf((512, 256), F32),
            buf((640, 128), F32),
            buf((16, *tile), F32),
            buf((2, *tile), F32), buf(tile, F32), buf((zs, *tile), F32),
            buf((2, *tile), F32), buf(tile, F32), buf((zs, *tile), F32),
            buf((32, *tile), F32),
            pltpu.SemaphoreType.REGULAR((3,)),
            dma((6,)), dma((2, 2, 3)), dma((2, 2, 3)), dma((2, 2, 3)), dma((2, 2, 3)),
            dma((16,)), dma((16,)), dma((2,)), dma((2,)), dma((2, zs)), dma((2, zs)), dma((32,)), dma((32,)),
        ],
        compiler_params=pltpu.CompilerParams(collective_id=0, has_side_effects=True, vmem_limit_bytes=32 << 20),
    )(
        *(
            pltpu.with_memory_space_constraint(a, pltpu.HBM)
            for a in (
                gate_grads, gate_rows.reshape(1, 128), gate_cols.reshape(32, 128),
                out_grads, out_rows.reshape(4, 128), out_cols.reshape(8, 128),
            )
        )
    )
    outs = pl.pallas_call(
        finish,
        out_shape=(
            jax.ShapeDtypeStruct((128, 4096), BF16),
            jax.ShapeDtypeStruct((1, 128), F32),
            jax.ShapeDtypeStruct((32, 128), F32),
            jax.ShapeDtypeStruct((512, 1024), BF16),
            jax.ShapeDtypeStruct((4, 128), F32),
            jax.ShapeDtypeStruct((8, 128), F32),
        ),
        in_specs=[vmem] * 9,
        out_specs=(hbm,) * 6,
        scratch_shapes=[buf((128, 4096), BF16), buf((512, 1024), BF16), dma((12,))],
        compiler_params=pltpu.CompilerParams(vmem_limit_bytes=32 << 20),
    )(*held)
    gate_up, gate_r, gate_c, out_up, out_r, out_c = outs
    return gate_up, gate_r.reshape(128), gate_c.reshape(4096), out_up, out_r.reshape(512), out_c.reshape(1024)


def solution(mesh):
    in_specs = (P("dp", "row", "col"), P("row"), P("col"), P("dp", "row", "col"), P("row"), P("col"))
    out_specs = (P("row", "col"), P("row"), P("col"), P("row", "col"), P("row"), P("col"))
    return jax.shard_map(
        functools.partial(local, mesh.shape["row"] // 2), mesh=mesh, in_specs=in_specs, out_specs=out_specs, check_vma=False
    )
```

```python
import functools

import jax
import jax.numpy as jnp
from jax import lax
from jax.experimental import pallas as pl
from jax.experimental.pallas import tpu as pltpu
from jax.sharding import PartitionSpec as P

D = 4096
FF = 16384
KEEP = 0.8
TINY = 1e-30
MESH = pl.DeviceIdType.MESH
F32 = jnp.float32
BF16 = jnp.bfloat16


class Mat:
    def __init__(self, rows, width, m, n, first_row):
        self.rows, self.width, self.m, self.n, self.first_row = rows, width, m, n, first_row
        self.chunk = width // 4
        self.half = rows // 2
        self.tiles = self.chunk // 128
        self.parts = max(1, self.half // 128)


GATE = Mat(128, 4096, D, FF, 0)
OUT = Mat(512, 1024, FF, D, 128)
MATS = (GATE, OUT)


def cols_of(mat, k):
    return pl.ds(pl.multiple_of(k * mat.chunk, 128), mat.chunk)


def half_of(mat, h):
    return pl.ds(h * mat.half, mat.half)


def rcopy(src, dst, send, recv, dev):
    return pltpu.make_async_remote_copy(
        src_ref=src, dst_ref=dst, send_sem=send, recv_sem=recv, device_id=dev, device_id_type=MESH
    )


def kernel(
    zs,
    gate_in, gate_rows_in, gate_cols_in, out_in, out_rows_in, out_cols_in,
    full_g, full_o, rmat, cf_g, cf_o, gate_rows_new, gate_cols_new, out_rows_new, out_cols_new,
    gate_rows, gate_cols, out_rows, out_cols,
    own_g, own_o, tr_g, tr_o, st_g, st_o, fr_g, fr_o,
    sq_g, sq_o, lanes, rows_buf, q_mine, q_sib, q_z, w_mine, w_sib, w_z, c_buf, e_buf,
    token, load_sem, rs_send, rs_recv, ag_send, ag_recv,
    s1_send, s1_recv, core_send, core_recv, z_send, z_recv, s2_send, s2_recv, s3_send, s3_recv,
):
    x, r, y = lax.axis_index("dp"), lax.axis_index("row"), lax.axis_index("col")
    z, core = r // 2, r % 2
    right, left, over = (x + 1) % 4, (x + 3) % 4, (x + 2) % 4
    dev = ((right, r, y), (left, r, y))
    sibling = (x, z * 2 + (1 - core), y)
    ins, own, tr, st, fr, full = (gate_in, out_in), (own_g, own_o), (tr_g, tr_o), (st_g, st_o), (fr_g, fr_o), (full_g, full_o)

    hops = lambda k, n: min(k, n - k)
    far = sorted(((i, j) for i in range(4) for j in range(4) if i or j), key=lambda p: -hops(p[0], 4) - hops(p[1], 4))
    xy_partners = [((x + i) % 4, (y + j) % 4) for i, j in far]
    z_partners = [(z + k) % zs for k in sorted(range(1, zs), key=lambda k: -hops(k, zs))]
    along_z = lambda k: (x, ((z + k + zs) % zs) * 2 + core, y)
    across_x, across_y = (over, r, y), (x, r, (y + 2) % 4)
    nearest = [dev[0], dev[1], (x, r, (y + 1) % 4), (x, r, (y + 3) % 4), along_z(1), along_z(-1), sibling]
    rounds = (nearest, [across_x, across_y, along_z(2), along_z(-2), sibling], [along_z(4), along_z(-4), across_x])

    def tell(k):
        for who in rounds[k]:
            pl.semaphore_signal(token.at[k], inc=1, device_id=who, device_id_type=MESH)

    def hear(k):
        pl.semaphore_wait(token.at[k], len(rounds[k]))

    barrier = pltpu.get_barrier_semaphore()
    for who in nearest:
        pl.semaphore_signal(barrier, inc=1, device_id=who, device_id_type=MESH)
    loads = [
        pltpu.make_async_copy(src, dst, load_sem.at[i])
        for i, (src, dst) in enumerate(
            (
                (gate_in.at[0], own_g), (out_in.at[0], own_o),
                (gate_rows_in, gate_rows), (gate_cols_in, gate_cols), (out_rows_in, out_rows), (out_cols_in, out_cols),
            )
        )
    ]
    for load in loads:
        load.start()

    q_mine[...] = jnp.zeros_like(q_mine)
    w_mine[...] = jnp.zeros_like(w_mine)
    pl.semaphore_wait(barrier, len(nearest))

    sends = []

    def go(copy):
        copy.start()
        sends.append(copy)

    def rs_transit(i, d):
        return rcopy(
            ins[i].at[0, half_of(MATS[i], d), cols_of(MATS[i], over)], tr[i].at[d],
            rs_send.at[i, d, 0], rs_recv.at[i, d, 0], dev[d],
        )

    def rs_alone(i, d):
        to = (right, left)[d]
        return rcopy(
            ins[i].at[0, half_of(MATS[i], 1 - d), cols_of(MATS[i], to)], fr[i].at[d, half_of(MATS[i], 1 - d)],
            rs_send.at[i, d, 1], rs_recv.at[i, d, 1], dev[d],
        )

    def rs_sum(i, d, p):
        size = MATS[i].half // MATS[i].parts
        return rcopy(
            st[i].at[d, pl.ds(p * size, size)], fr[i].at[d, pl.ds(d * MATS[i].half + p * size, size)],
            rs_send.at[i, d, 2 + p], rs_recv.at[i, d, 2 + p], dev[d],
        )

    for make in (rs_transit, rs_alone):
        for i in range(2):
            for d in range(2):
                go(make(i, d))
    tell(0)
    for load in loads:
        load.wait()
    for i in range(2):
        mat = MATS[i]
        for d in range(2):
            to = (right, left)[d]
            rs_transit(i, d).wait_recv()
            step = 16384 // mat.chunk

            def add(n, _, i=i, d=d, to=to, mat=mat, step=step):
                rows = pl.ds(pl.multiple_of(n * step, 16), step)
                mine = own[i][pl.ds(pl.multiple_of(d * mat.half + n * step, 16), step), cols_of(mat, to)]
                st[i][d, rows, :] = (mine.astype(F32) + tr[i][d, rows, :].astype(F32)).astype(BF16)
                return 0

            lax.fori_loop(0, mat.half // step, add, 0)
            for p in range(mat.parts):
                go(rs_sum(i, d, p))
        hear(i)
        tell(i + 1)

    def ag_own(i, d, p):
        h = d if p == 0 else 1 - d
        ref = full[i].at[half_of(MATS[i], h), cols_of(MATS[i], x)]
        return rcopy(ref, ref, ag_send.at[i, d, p], ag_recv.at[i, d, p], dev[d])

    def ag_landed(i, d, p):
        h = d if p != 1 else 1 - d
        k = over if p == 2 else (left, right)[d]
        ref = full[i].at[half_of(MATS[i], h), cols_of(MATS[i], k)]
        return rcopy(ref, ref, ag_send.at[i, d, p], ag_recv.at[i, d, p], dev[d])

    def ag_forward(i, d):
        ref = full[i].at[half_of(MATS[i], d), cols_of(MATS[i], (left, right)[d])]
        return rcopy(ref, ref, ag_send.at[i, d, 2], ag_recv.at[i, d, 2], dev[d])

    me_xy = x * 4 + y
    for i in range(2):
        mat = MATS[i]
        sq = (sq_g, sq_o)[i]
        for d in range(2):
            rs_alone(i, d).wait_recv()
        step = 16384 // mat.chunk

        def total(n, acc, i=i, mat=mat, sq=sq, step=step):
            rows = pl.ds(n * step, step)
            s = own[i][rows, cols_of(mat, x)].astype(F32) + fr[i][0, rows, :].astype(F32) + fr[i][1, rows, :].astype(F32)
            full[i][rows, cols_of(mat, x)] = s.astype(BF16)
            s = s * s
            sq[rows, :] = s
            by_lane = s[:, 0:128]
            for t in range(1, mat.tiles):
                by_lane = by_lane + s[:, t * 128 : (t + 1) * 128]
            lanes[pl.ds(mat.first_row + n * step, step), :] = by_lane
            for k in range(step // 8):
                acc = acc + s[k * 8 : (k + 1) * 8, :]
            return acc

        acc = jnp.zeros((8, mat.chunk), F32)
        size = mat.half // mat.parts
        for p in range(mat.parts):
            for d in range(2):
                rs_sum(i, d, p).wait_recv()
            for d in range(2):
                first = d * mat.half + p * size
                for n in range(first // step, (first + size) // step):
                    acc = total(n, acc)
                if mat.parts > 1 or d == 1:
                    b = (mat.first_row + first) // 128
                    block = lanes[b * 128 : (b + 1) * 128, :].T
                    rows_buf[me_xy, b : b + 1, :] = jnp.sum(block, axis=0, keepdims=True)
        if i == 0:
            for d in range(2):
                go(ag_own(i, d, 0))
        col = jnp.sum(acc, axis=0, keepdims=True)
        for h in range(2):
            for t in range(mat.tiles // 2):
                k = h * (mat.tiles // 2) + t
                at = t if i == 0 else 4
                q_mine[h, at : at + 1, :] = col[:, k * 128 : (k + 1) * 128]

    hear(2)
    def s1(a, b, peer):
        return rcopy(
            rows_buf.at[me_xy if peer is None else peer, pl.ds(0, 5)], rows_buf.at[me_xy if peer is None else peer, pl.ds(0, 5)],
            s1_send.at[a * 4 + b], s1_recv.at[me_xy if peer is None else peer], (a, r, b),
        )

    for a, b in xy_partners:
        go(s1(a, b, None))

    def to_core(buf, got, j):
        return rcopy(buf.at[1 - core], got, core_send.at[j], core_recv.at[j], sibling)


    for i, p in ((1, 0), (0, 1), (1, 1)):
        for d in range(2):
            go(ag_own(i, d, p))
        if (i, p) == (1, 0):
            go(to_core(q_mine, q_sib, 0))

    def to_z(buf, j, k, peer):
        slot = z if peer is None else peer
        rows = pl.ds(0, (5, 16)[j])
        return rcopy(
            buf.at[slot, rows], buf.at[slot, rows], z_send.at[j, k], z_recv.at[j, slot], (x, k * 2 + core, y)
        )

    to_core(q_mine, q_sib, 0).wait_recv()
    q_z[z] = q_mine[core] + q_sib[...]
    for k in z_partners:
        go(to_z(q_z, 0, k, None))

    for a, b in xy_partners[::-1]:
        s1(a, b, a * 4 + b).wait_recv()
    row_sum = rows_buf[0, 0:5, :]
    for k in range(1, 16):
        row_sum = row_sum + rows_buf[k, 0:5, :]
    g_rows = KEEP * gate_rows[...] + (1.0 - KEEP) * (row_sum[0:1] * (1.0 / FF) + TINY)
    o_rows = KEEP * out_rows[...] + (1.0 - KEEP) * (row_sum[1:5] * (1.0 / D) + TINY)
    gate_rows_new[...] = g_rows
    out_rows_new[...] = o_rows
    for b in range(5):
        one = g_rows if b == 0 else o_rows[b - 1 : b]
        rmat[b * 128 : (b + 1) * 128, :] = jnp.broadcast_to(lax.rsqrt(one), (128, 128)).T

    for i in range(2):
        mat = MATS[i]
        sq = (sq_g, sq_o)[i]
        step = 16384 // mat.chunk

        def weigh(n, acc, mat=mat, sq=sq, step=step):
            f = rmat[pl.ds(pl.multiple_of(mat.first_row + n * step, 8), step), :]
            f = f * f
            out = []
            for t in range(mat.tiles):
                p = sq[pl.ds(pl.multiple_of(n * step, 8), step), t * 128 : (t + 1) * 128] * f
                a = acc[t]
                for k in range(step // 8):
                    a = a + p[k * 8 : (k + 1) * 8, :]
                out.append(a)
            return tuple(out)

        acc = lax.fori_loop(0, mat.rows // step, weigh, tuple(jnp.zeros((8, 128), F32) for _ in range(mat.tiles)))
        for t in range(mat.tiles):
            at = t if i == 0 else 8 + t
            w_mine[at : at + 1, :] = jnp.sum(acc[t], axis=0, keepdims=True)
    for at in (10, 12):
        w_mine[at : at + 1, :] = g_rows
        w_mine[at + 1 : at + 2, :] = jnp.sum(o_rows, axis=0, keepdims=True)
    w_pair = rcopy(w_mine, w_sib, core_send.at[1], core_recv.at[1], sibling)
    go(w_pair)
    w_pair.wait_recv()
    w = w_mine[...] + w_sib[...]
    w = jnp.where(lax.broadcasted_iota(jnp.int32, w.shape, 0) >= 12, w - w.astype(BF16).astype(F32), w)
    w_z[z] = w.astype(BF16)
    for k in z_partners:
        go(to_z(w_z, 1, k, None))

    for i in (0,):
        for d in range(2):
            ag_landed(i, d, 0).wait_recv()
            go(ag_forward(i, d))

    for k in z_partners[::-1]:
        to_z(q_z, 0, k, k).wait_recv()
    q = q_z[0]
    for k in range(1, zs):
        q = q + q_z[k]
    old_g = gate_cols[pl.ds(pl.multiple_of(x * 8 + core * 4, 4), 4), :]
    old_o = out_cols[pl.ds(x * 2 + core, 1), :]
    c_g = KEEP * old_g + (1.0 - KEEP) * (q[0:4] * (1.0 / D) + TINY)
    c_o = KEEP * old_o + (1.0 - KEEP) * (q[4:5] * (1.0 / FF) + TINY)
    me_c = x * 2 + core
    c_buf[me_c, 0:4, :] = c_g
    c_buf[me_c, 4:5, :] = c_o

    def s2(a, h, peer):
        slot = me_c if peer is None else peer
        part = c_buf.at[slot, pl.ds(0, 5)]
        return rcopy(part, part, s2_send.at[a * 2 + h], s2_recv.at[slot], (a, z * 2 + h, y))

    c_partners = [(over, 1 - core), (over, core), (right, 1 - core), (left, 1 - core), (right, core), (left, core), (x, 1 - core)]
    for a, h in c_partners:
        go(s2(a, h, None))
    for i in (1,):
        for d in range(2):
            ag_landed(i, d, 0).wait_recv()
            go(ag_forward(i, d))

    s2(x, 1 - core, x * 2 + 1 - core).wait_recv()
    inv = [1.0 / c_buf[x * 2 + h, 0:5, :] for h in range(2)]
    for k in z_partners[::-1]:
        to_z(w_z, 1, k, k).wait_recv()
    w = w_z[0].astype(F32)
    for k in range(1, zs):
        w = w + w_z[k].astype(F32)

    e_buf[me_xy, 0:1, :] = jnp.sum(w[0:4] * inv[0][0:4] + w[4:8] * inv[1][0:4], axis=0, keepdims=True)
    e_buf[me_xy, 1:2, :] = w[8:9] * inv[0][4:5] + w[9:10] * inv[1][4:5]

    def s3(a, b, peer):
        slot = me_xy if peer is None else peer
        part = e_buf.at[slot, pl.ds(0, 2)]
        return rcopy(part, part, s3_send.at[a * 4 + b], s3_recv.at[slot], (a, r, b))

    for a, b in xy_partners:
        go(s3(a, b, None))

    means = [jnp.sum(w[10 + i : 11 + i] + w[12 + i : 13 + i], axis=1, keepdims=True) * (1.0 / MATS[i].m) for i in range(2)]
    for a, h in c_partners[-2::-1]:
        s2(a, h, a * 2 + h).wait_recv()
    for k in range(4):
        for h in range(2):
            slot = k * 2 + h
            gate_cols_new[8 * k + 4 * h : 8 * k + 4 * h + 4, :] = c_buf[slot, 0:4, :]
            out_cols_new[2 * k + h : 2 * k + h + 1, :] = c_buf[slot, 4:5, :]
    cf_g[...] = lax.rsqrt(gate_cols_new[...])
    cf_o[...] = lax.rsqrt(out_cols_new[...])
    for i in range(2):
        for d in range(2):
            for p in (1, 2):
                ag_landed(i, d, p).wait_recv()
    for copy in sends:
        copy.wait_send()
    for a, b in xy_partners[::-1]:
        s3(a, b, a * 4 + b).wait_recv()
    e = e_buf[0, 0:2, :]
    for k in range(1, 16):
        e = e + e_buf[k, 0:2, :]
    for i in range(2):
        energy = jnp.sum(e[i : i + 1], axis=1, keepdims=True)
        root = jnp.sqrt(means[i] * (energy * (1.0 / (D * FF))))
        factor = jnp.sqrt(means[i]) / jnp.maximum(1.0, root)
        cf = (cf_g, cf_o)[i]
        cf[...] = cf[...] * factor


def finish(
    full_g, full_o, rmat, cf_g, cf_o, gate_r, gate_c, out_r, out_c,
    gate_up, gate_rows_new, gate_cols_new, out_up, out_rows_new, out_cols_new,
    res_g, res_o, store_sem,
):
    stores = []

    def store(src, dst):
        stores.append(pltpu.make_async_copy(src, dst, store_sem.at[len(stores)]))
        stores[-1].start()

    store(gate_r, gate_rows_new)
    store(gate_c, gate_cols_new)
    store(out_r, out_rows_new)
    store(out_c, out_cols_new)
    for k in range(4):

        def scale(t, _, k=k):
            cols = pl.ds(pl.multiple_of((k * 8 + t) * 128, 128), 128)
            res_g[:, cols] = (full_g[:, cols].astype(F32) * rmat[0:128, :] * cf_g[pl.ds(k * 8 + t, 1), :]).astype(BF16)
            return 0

        lax.fori_loop(0, 8, scale, 0, unroll=True)
        part = pl.ds(k * 1024, 1024)
        store(res_g.at[:, part], gate_up.at[:, part])
    for k in range(4):

        def scale(t, _, k=k):
            cols = pl.ds(pl.multiple_of(t * 128, 128), 128)
            rows = pl.ds(k * 128, 128)
            by_row = rmat[(k + 1) * 128 : (k + 2) * 128, :]
            res_o[rows, cols] = (full_o[rows, cols].astype(F32) * by_row * cf_o[pl.ds(t, 1), :]).astype(BF16)
            return 0

        lax.fori_loop(0, 8, scale, 0, unroll=True)
        part = pl.ds(k * 128, 128)
        store(res_o.at[part], out_up.at[part])
    for copy in stores:
        copy.wait()


def local(zs, gate_grads, gate_rows, gate_cols, out_grads, out_rows, out_cols):
    vmem, hbm = pl.BlockSpec(memory_space=pltpu.VMEM), pl.BlockSpec(memory_space=pltpu.HBM)
    dma, buf = pltpu.SemaphoreType.DMA, pltpu.VMEM
    tile = (8, 128)
    held = pl.pallas_call(
        functools.partial(kernel, zs),
        out_shape=(
            jax.ShapeDtypeStruct((128, 4096), BF16),
            jax.ShapeDtypeStruct((512, 1024), BF16),
            jax.ShapeDtypeStruct((640, 128), F32),
            jax.ShapeDtypeStruct((32, 128), F32),
            jax.ShapeDtypeStruct((8, 128), F32),
            jax.ShapeDtypeStruct((1, 128), F32),
            jax.ShapeDtypeStruct((32, 128), F32),
            jax.ShapeDtypeStruct((4, 128), F32),
            jax.ShapeDtypeStruct((8, 128), F32),
        ),
        in_specs=[hbm] * 6,
        out_specs=(vmem,) * 9,
        scratch_shapes=[
            buf((1, 128), F32), buf((32, 128), F32), buf((4, 128), F32), buf((8, 128), F32),
            buf((128, 4096), BF16), buf((512, 1024), BF16),
            buf((2, 64, 1024), BF16), buf((2, 256, 256), BF16),
            buf((2, 64, 1024), BF16), buf((2, 256, 256), BF16),
            buf((2, 128, 1024), BF16), buf((2, 512, 256), BF16),
            buf((128, 1024), F32), buf((512, 256), F32),
            buf((640, 128), F32),
            buf((16, *tile), F32),
            buf((2, *tile), F32), buf(tile, F32), buf((zs, *tile), F32),
            buf((16, 128), F32), buf((16, 128), F32), buf((zs, 16, 128), BF16),
            buf((8, *tile), F32), buf((16, *tile), F32),
            pltpu.SemaphoreType.REGULAR((3,)),
            dma((6,)), dma((2, 2, 4)), dma((2, 2, 4)), dma((2, 2, 3)), dma((2, 2, 3)),
            dma((16,)), dma((16,)), dma((2,)), dma((2,)), dma((2, zs)), dma((2, zs)), dma((8,)), dma((8,)), dma((16,)), dma((16,)),
        ],
        compiler_params=pltpu.CompilerParams(collective_id=0, has_side_effects=True, vmem_limit_bytes=32 << 20),
    )(
        *(
            pltpu.with_memory_space_constraint(a, pltpu.HBM)
            for a in (
                gate_grads, gate_rows.reshape(1, 128), gate_cols.reshape(32, 128),
                out_grads, out_rows.reshape(4, 128), out_cols.reshape(8, 128),
            )
        )
    )
    outs = pl.pallas_call(
        finish,
        out_shape=(
            jax.ShapeDtypeStruct((128, 4096), BF16),
            jax.ShapeDtypeStruct((1, 128), F32),
            jax.ShapeDtypeStruct((32, 128), F32),
            jax.ShapeDtypeStruct((512, 1024), BF16),
            jax.ShapeDtypeStruct((4, 128), F32),
            jax.ShapeDtypeStruct((8, 128), F32),
        ),
        in_specs=[vmem] * 9,
        out_specs=(hbm,) * 6,
        scratch_shapes=[buf((128, 4096), BF16), buf((512, 1024), BF16), dma((12,))],
        compiler_params=pltpu.CompilerParams(vmem_limit_bytes=32 << 20),
    )(*held)
    gate_up, gate_r, gate_c, out_up, out_r, out_c = outs
    return gate_up, gate_r.reshape(128), gate_c.reshape(4096), out_up, out_r.reshape(512), out_c.reshape(1024)


def solution(mesh):
    in_specs = (P("dp", "row", "col"), P("row"), P("col"), P("dp", "row", "col"), P("row"), P("col"))
    out_specs = (P("row", "col"), P("row"), P("col"), P("row", "col"), P("row"), P("col"))
    return jax.shard_map(
        functools.partial(local, mesh.shape["row"] // 2), mesh=mesh, in_specs=in_specs, out_specs=out_specs, check_vma=False
    )
```

```python
import functools

import jax
import jax.numpy as jnp
from jax import lax
from jax.experimental import pallas as pl
from jax.experimental.pallas import tpu as pltpu
from jax.sharding import PartitionSpec as P

D = 4096
FF = 16384
KEEP = 0.8
TINY = 1e-30
MESH = pl.DeviceIdType.MESH
F32 = jnp.float32
BF16 = jnp.bfloat16


class Mat:
    def __init__(self, rows, width, m, n, first_row):
        self.rows, self.width, self.m, self.n, self.first_row = rows, width, m, n, first_row
        self.chunk = width // 4
        self.half = rows // 2
        self.tiles = self.chunk // 128
        self.parts = max(1, self.half // 128)


GATE = Mat(128, 4096, D, FF, 0)
OUT = Mat(512, 1024, FF, D, 128)
MATS = (GATE, OUT)


def cols_of(mat, k):
    return pl.ds(pl.multiple_of(k * mat.chunk, 128), mat.chunk)


def half_of(mat, h):
    return pl.ds(h * mat.half, mat.half)


def rcopy(src, dst, send, recv, dev):
    return pltpu.make_async_remote_copy(
        src_ref=src, dst_ref=dst, send_sem=send, recv_sem=recv, device_id=dev, device_id_type=MESH
    )


def kernel(
    zs,
    gate_in, gate_rows_in, gate_cols_in, out_in, out_rows_in, out_cols_in,
    full_g, full_o, rmat, cf_g, cf_o, gate_rows_new, gate_cols_new, out_rows_new, out_cols_new,
    gate_rows, gate_cols, out_rows, out_cols,
    own_g, own_o, tr_g, tr_o, st_g, st_o, fr_g, fr_o,
    sq_g, sq_o, lanes, rows_buf, q_mine, q_sib, q_z, w_mine, w_sib, w_z, c_buf, e_buf,
    token, load_sem, rs_send, rs_recv, ag_send, ag_recv,
    s1_send, s1_recv, core_send, core_recv, z_send, z_recv, s2_send, s2_recv, s3_send, s3_recv,
):
    x, r, y = lax.axis_index("dp"), lax.axis_index("row"), lax.axis_index("col")
    z, core = r // 2, r % 2
    right, left, over = (x + 1) % 4, (x + 3) % 4, (x + 2) % 4
    dev = ((right, r, y), (left, r, y))
    sibling = (x, z * 2 + (1 - core), y)
    ins, own, tr, st, fr, full = (gate_in, out_in), (own_g, own_o), (tr_g, tr_o), (st_g, st_o), (fr_g, fr_o), (full_g, full_o)

    hops = lambda k, n: min(k, n - k)
    far = sorted(((i, j) for i in range(4) for j in range(4) if i or j), key=lambda p: -hops(p[0], 4) - hops(p[1], 4))
    xy_partners = [((x + i) % 4, (y + j) % 4) for i, j in far]
    z_partners = [(z + k) % zs for k in sorted(range(1, zs), key=lambda k: -hops(k, zs))]
    along_z = lambda k: (x, ((z + k + zs) % zs) * 2 + core, y)
    across_x, across_y = (over, r, y), (x, r, (y + 2) % 4)
    nearest = [dev[0], dev[1], (x, r, (y + 1) % 4), (x, r, (y + 3) % 4), along_z(1), along_z(-1), sibling]
    rounds = (nearest, [across_x, across_y, along_z(2), along_z(-2), sibling], [along_z(4), along_z(-4), across_x])

    def tell(k):
        for who in rounds[k]:
            pl.semaphore_signal(token.at[k], inc=1, device_id=who, device_id_type=MESH)

    def hear(k):
        pl.semaphore_wait(token.at[k], len(rounds[k]))

    barrier = pltpu.get_barrier_semaphore()
    for who in nearest:
        pl.semaphore_signal(barrier, inc=1, device_id=who, device_id_type=MESH)
    loads = [
        pltpu.make_async_copy(src, dst, load_sem.at[i])
        for i, (src, dst) in enumerate(
            (
                (gate_in.at[0], own_g), (out_in.at[0], own_o),
                (gate_rows_in, gate_rows), (gate_cols_in, gate_cols), (out_rows_in, out_rows), (out_cols_in, out_cols),
            )
        )
    ]
    for load in loads:
        load.start()

    q_mine[...] = jnp.zeros_like(q_mine)
    w_mine[...] = jnp.zeros_like(w_mine)
    pl.semaphore_wait(barrier, len(nearest))

    sends = []

    def go(copy):
        copy.start()
        sends.append(copy)

    def rs_transit(i, d):
        return rcopy(
            ins[i].at[0, half_of(MATS[i], d), cols_of(MATS[i], over)], tr[i].at[d],
            rs_send.at[i, d, 0], rs_recv.at[i, d, 0], dev[d],
        )

    def rs_alone(i, d):
        to = (right, left)[d]
        return rcopy(
            ins[i].at[0, half_of(MATS[i], 1 - d), cols_of(MATS[i], to)], fr[i].at[d, half_of(MATS[i], 1 - d)],
            rs_send.at[i, d, 1], rs_recv.at[i, d, 1], dev[d],
        )

    def rs_sum(i, d, p):
        size = MATS[i].half // MATS[i].parts
        return rcopy(
            st[i].at[d, pl.ds(p * size, size)], fr[i].at[d, pl.ds(d * MATS[i].half + p * size, size)],
            rs_send.at[i, d, 2 + p], rs_recv.at[i, d, 2 + p], dev[d],
        )

    for make in (rs_transit, rs_alone):
        for i in range(2):
            for d in range(2):
                go(make(i, d))
    tell(0)
    for load in loads:
        load.wait()
    for i in range(2):
        mat = MATS[i]
        for d in range(2):
            to = (right, left)[d]
            rs_transit(i, d).wait_recv()
            step = 16384 // mat.chunk

            def add(n, _, i=i, d=d, to=to, mat=mat, step=step):
                rows = pl.ds(pl.multiple_of(n * step, 16), step)
                mine = own[i][pl.ds(pl.multiple_of(d * mat.half + n * step, 16), step), cols_of(mat, to)]
                st[i][d, rows, :] = (mine.astype(F32) + tr[i][d, rows, :].astype(F32)).astype(BF16)
                return 0

            lax.fori_loop(0, mat.half // step, add, 0)
            for p in range(mat.parts):
                go(rs_sum(i, d, p))
        hear(i)
        tell(i + 1)

    def ag_own(i, d, p):
        h = d if p == 0 else 1 - d
        ref = full[i].at[half_of(MATS[i], h), cols_of(MATS[i], x)]
        return rcopy(ref, ref, ag_send.at[i, d, p], ag_recv.at[i, d, p], dev[d])

    def ag_landed(i, d, p):
        h = d if p != 1 else 1 - d
        k = over if p == 2 else (left, right)[d]
        ref = full[i].at[half_of(MATS[i], h), cols_of(MATS[i], k)]
        return rcopy(ref, ref, ag_send.at[i, d, p], ag_recv.at[i, d, p], dev[d])

    def ag_forward(i, d):
        ref = full[i].at[half_of(MATS[i], d), cols_of(MATS[i], (left, right)[d])]
        return rcopy(ref, ref, ag_send.at[i, d, 2], ag_recv.at[i, d, 2], dev[d])

    me_xy = x * 4 + y
    for i in range(2):
        mat = MATS[i]
        sq = (sq_g, sq_o)[i]
        for d in range(2):
            rs_alone(i, d).wait_recv()
        step = 16384 // mat.chunk

        def total(n, acc, i=i, mat=mat, sq=sq, step=step):
            rows = pl.ds(n * step, step)
            s = own[i][rows, cols_of(mat, x)].astype(F32) + fr[i][0, rows, :].astype(F32) + fr[i][1, rows, :].astype(F32)
            full[i][rows, cols_of(mat, x)] = s.astype(BF16)
            s = s * s
            sq[rows, :] = s
            by_lane = s[:, 0:128]
            for t in range(1, mat.tiles):
                by_lane = by_lane + s[:, t * 128 : (t + 1) * 128]
            lanes[pl.ds(mat.first_row + n * step, step), :] = by_lane
            for k in range(step // 8):
                acc = acc + s[k * 8 : (k + 1) * 8, :]
            return acc

        acc = jnp.zeros((8, mat.chunk), F32)
        size = mat.half // mat.parts
        for p in range(mat.parts):
            for d in range(2):
                rs_sum(i, d, p).wait_recv()
            for d in range(2):
                first = d * mat.half + p * size
                for n in range(first // step, (first + size) // step):
                    acc = total(n, acc)
                if mat.parts > 1 or d == 1:
                    b = (mat.first_row + first) // 128
                    block = lanes[b * 128 : (b + 1) * 128, :].T
                    rows_buf[me_xy, b : b + 1, :] = jnp.sum(block, axis=0, keepdims=True)
        if i == 0:
            for d in range(2):
                go(ag_own(i, d, 0))
        col = jnp.sum(acc, axis=0, keepdims=True)
        for h in range(2):
            for t in range(mat.tiles // 2):
                k = h * (mat.tiles // 2) + t
                at = t if i == 0 else 4
                q_mine[h, at : at + 1, :] = col[:, k * 128 : (k + 1) * 128]

    hear(2)
    def s1(a, b, peer):
        return rcopy(
            rows_buf.at[me_xy if peer is None else peer, pl.ds(0, 5)], rows_buf.at[me_xy if peer is None else peer, pl.ds(0, 5)],
            s1_send.at[a * 4 + b], s1_recv.at[me_xy if peer is None else peer], (a, r, b),
        )

    for a, b in xy_partners:
        go(s1(a, b, None))

    def to_core(buf, got, j):
        return rcopy(buf.at[1 - core], got, core_send.at[j], core_recv.at[j], sibling)


    for i, p in ((1, 0), (0, 1), (1, 1)):
        for d in range(2):
            go(ag_own(i, d, p))
        if (i, p) == (1, 0):
            go(to_core(q_mine, q_sib, 0))

    def to_z(buf, j, k, peer):
        slot = z if peer is None else peer
        rows = pl.ds(0, (5, 16)[j])
        return rcopy(
            buf.at[slot, rows], buf.at[slot, rows], z_send.at[j, k], z_recv.at[j, slot], (x, k * 2 + core, y)
        )

    to_core(q_mine, q_sib, 0).wait_recv()
    q_z[z] = q_mine[core] + q_sib[...]
    for k in z_partners:
        go(to_z(q_z, 0, k, None))

    for a, b in xy_partners[::-1]:
        s1(a, b, a * 4 + b).wait_recv()
    row_sum = rows_buf[0, 0:5, :]
    for k in range(1, 16):
        row_sum = row_sum + rows_buf[k, 0:5, :]
    g_rows = KEEP * gate_rows[...] + (1.0 - KEEP) * (row_sum[0:1] * (1.0 / FF) + TINY)
    o_rows = KEEP * out_rows[...] + (1.0 - KEEP) * (row_sum[1:5] * (1.0 / D) + TINY)
    gate_rows_new[...] = g_rows
    out_rows_new[...] = o_rows
    for b in range(5):
        one = g_rows if b == 0 else o_rows[b - 1 : b]
        rmat[b * 128 : (b + 1) * 128, :] = jnp.broadcast_to(lax.rsqrt(one), (128, 128)).T

    for i in range(2):
        mat = MATS[i]
        sq = (sq_g, sq_o)[i]
        step = 16384 // mat.chunk

        def weigh(n, acc, mat=mat, sq=sq, step=step):
            f = rmat[pl.ds(pl.multiple_of(mat.first_row + n * step, 8), step), :]
            f = f * f
            out = []
            for t in range(mat.tiles):
                p = sq[pl.ds(pl.multiple_of(n * step, 8), step), t * 128 : (t + 1) * 128] * f
                a = acc[t]
                for k in range(step // 8):
                    a = a + p[k * 8 : (k + 1) * 8, :]
                out.append(a)
            return tuple(out)

        acc = lax.fori_loop(0, mat.rows // step, weigh, tuple(jnp.zeros((8, 128), F32) for _ in range(mat.tiles)))
        for t in range(mat.tiles):
            at = t if i == 0 else 8 + t
            w_mine[at : at + 1, :] = jnp.sum(acc[t], axis=0, keepdims=True)
    for at in (10, 12):
        w_mine[at : at + 1, :] = g_rows
        w_mine[at + 1 : at + 2, :] = jnp.sum(o_rows, axis=0, keepdims=True)
    w_pair = rcopy(w_mine, w_sib, core_send.at[1], core_recv.at[1], sibling)
    go(w_pair)
    w_pair.wait_recv()
    w = w_mine[...] + w_sib[...]
    w = jnp.where(lax.broadcasted_iota(jnp.int32, w.shape, 0) >= 12, w - w.astype(BF16).astype(F32), w)
    w_z[z] = w.astype(BF16)
    for k in z_partners:
        go(to_z(w_z, 1, k, None))

    for i in (0,):
        for d in range(2):
            ag_landed(i, d, 0).wait_recv()
            go(ag_forward(i, d))

    for k in z_partners[::-1]:
        to_z(q_z, 0, k, k).wait_recv()
    q = q_z[0]
    for k in range(1, zs):
        q = q + q_z[k]
    old_g = gate_cols[pl.ds(pl.multiple_of(x * 8, 8), 8), :]
    old_g = jnp.where(core == 0, old_g[0:4], old_g[4:8])
    mine = lax.broadcasted_iota(jnp.int32, (8, 128), 0) == x * 2 + core
    old_o = jnp.sum(jnp.where(mine, out_cols[...], 0.0), axis=0, keepdims=True)
    c_g = KEEP * old_g + (1.0 - KEEP) * (q[0:4] * (1.0 / D) + TINY)
    c_o = KEEP * old_o + (1.0 - KEEP) * (q[4:5] * (1.0 / FF) + TINY)
    me_c = x * 2 + core
    c_buf[me_c, 0:4, :] = c_g
    c_buf[me_c, 4:5, :] = c_o

    def s2(a, h, peer):
        slot = me_c if peer is None else peer
        part = c_buf.at[slot, pl.ds(0, 5)]
        return rcopy(part, part, s2_send.at[a * 2 + h], s2_recv.at[slot], (a, z * 2 + h, y))

    c_partners = [(over, 1 - core), (over, core), (right, 1 - core), (left, 1 - core), (right, core), (left, core), (x, 1 - core)]
    for a, h in c_partners:
        go(s2(a, h, None))
    for i in (1,):
        for d in range(2):
            ag_landed(i, d, 0).wait_recv()
            go(ag_forward(i, d))

    s2(x, 1 - core, x * 2 + 1 - core).wait_recv()
    inv = [1.0 / c_buf[x * 2 + h, 0:5, :] for h in range(2)]
    for k in z_partners[::-1]:
        to_z(w_z, 1, k, k).wait_recv()
    w = w_z[0].astype(F32)
    for k in range(1, zs):
        w = w + w_z[k].astype(F32)

    e_buf[me_xy, 0:1, :] = jnp.sum(w[0:4] * inv[0][0:4] + w[4:8] * inv[1][0:4], axis=0, keepdims=True)
    e_buf[me_xy, 1:2, :] = w[8:9] * inv[0][4:5] + w[9:10] * inv[1][4:5]

    def s3(a, b, peer):
        slot = me_xy if peer is None else peer
        part = e_buf.at[slot, pl.ds(0, 2)]
        return rcopy(part, part, s3_send.at[a * 4 + b], s3_recv.at[slot], (a, r, b))

    for a, b in xy_partners:
        go(s3(a, b, None))

    means = [jnp.sum(w[10 + i : 11 + i] + w[12 + i : 13 + i], axis=1, keepdims=True) * (1.0 / MATS[i].m) for i in range(2)]
    for a, h in c_partners[-2::-1]:
        s2(a, h, a * 2 + h).wait_recv()
    for k in range(4):
        for h in range(2):
            slot = k * 2 + h
            gate_cols_new[8 * k + 4 * h : 8 * k + 4 * h + 4, :] = c_buf[slot, 0:4, :]
            out_cols_new[2 * k + h : 2 * k + h + 1, :] = c_buf[slot, 4:5, :]
    cf_g[...] = lax.rsqrt(gate_cols_new[...])
    cf_o[...] = lax.rsqrt(out_cols_new[...])
    for i in range(2):
        for d in range(2):
            for p in (1, 2):
                ag_landed(i, d, p).wait_recv()
    for copy in sends:
        copy.wait_send()
    for a, b in xy_partners[::-1]:
        s3(a, b, a * 4 + b).wait_recv()
    e = e_buf[0, 0:2, :]
    for k in range(1, 16):
        e = e + e_buf[k, 0:2, :]
    for i in range(2):
        energy = jnp.sum(e[i : i + 1], axis=1, keepdims=True)
        root = jnp.sqrt(means[i] * (energy * (1.0 / (D * FF))))
        factor = jnp.sqrt(means[i]) / jnp.maximum(1.0, root)
        cf = (cf_g, cf_o)[i]
        cf[...] = cf[...] * factor


def finish(
    full_g, full_o, rmat, cf_g, cf_o, gate_r, gate_c, out_r, out_c,
    gate_up, gate_rows_new, gate_cols_new, out_up, out_rows_new, out_cols_new,
    res_g, res_o, store_sem,
):
    stores = []

    def store(src, dst):
        stores.append(pltpu.make_async_copy(src, dst, store_sem.at[len(stores)]))
        stores[-1].start()

    store(gate_r, gate_rows_new)
    store(gate_c, gate_cols_new)
    store(out_r, out_rows_new)
    store(out_c, out_cols_new)
    for k in range(4):

        def scale(t, _, k=k):
            cols = pl.ds(pl.multiple_of((k * 8 + t) * 128, 128), 128)
            res_g[:, cols] = (full_g[:, cols].astype(F32) * rmat[0:128, :] * cf_g[pl.ds(k * 8 + t, 1), :]).astype(BF16)
            return 0

        lax.fori_loop(0, 8, scale, 0, unroll=True)
        part = pl.ds(k * 1024, 1024)
        store(res_g.at[:, part], gate_up.at[:, part])
    for k in range(4):

        def scale(t, _, k=k):
            cols = pl.ds(pl.multiple_of(t * 128, 128), 128)
            rows = pl.ds(k * 128, 128)
            by_row = rmat[(k + 1) * 128 : (k + 2) * 128, :]
            res_o[rows, cols] = (full_o[rows, cols].astype(F32) * by_row * cf_o[pl.ds(t, 1), :]).astype(BF16)
            return 0

        lax.fori_loop(0, 8, scale, 0, unroll=True)
        part = pl.ds(k * 128, 128)
        store(res_o.at[part], out_up.at[part])
    for copy in stores:
        copy.wait()


def local(zs, gate_grads, gate_rows, gate_cols, out_grads, out_rows, out_cols):
    vmem, hbm = pl.BlockSpec(memory_space=pltpu.VMEM), pl.BlockSpec(memory_space=pltpu.HBM)
    dma, buf = pltpu.SemaphoreType.DMA, pltpu.VMEM
    tile = (8, 128)
    held = pl.pallas_call(
        functools.partial(kernel, zs),
        out_shape=(
            jax.ShapeDtypeStruct((128, 4096), BF16),
            jax.ShapeDtypeStruct((512, 1024), BF16),
            jax.ShapeDtypeStruct((640, 128), F32),
            jax.ShapeDtypeStruct((32, 128), F32),
            jax.ShapeDtypeStruct((8, 128), F32),
            jax.ShapeDtypeStruct((1, 128), F32),
            jax.ShapeDtypeStruct((32, 128), F32),
            jax.ShapeDtypeStruct((4, 128), F32),
            jax.ShapeDtypeStruct((8, 128), F32),
        ),
        in_specs=[hbm] * 6,
        out_specs=(vmem,) * 9,
        scratch_shapes=[
            buf((1, 128), F32), buf((32, 128), F32), buf((4, 128), F32), buf((8, 128), F32),
            buf((128, 4096), BF16), buf((512, 1024), BF16),
            buf((2, 64, 1024), BF16), buf((2, 256, 256), BF16),
            buf((2, 64, 1024), BF16), buf((2, 256, 256), BF16),
            buf((2, 128, 1024), BF16), buf((2, 512, 256), BF16),
            buf((128, 1024), F32), buf((512, 256), F32),
            buf((640, 128), F32),
            buf((16, *tile), F32),
            buf((2, *tile), F32), buf(tile, F32), buf((zs, *tile), F32),
            buf((16, 128), F32), buf((16, 128), F32), buf((zs, 16, 128), BF16),
            buf((8, *tile), F32), buf((16, *tile), F32),
            pltpu.SemaphoreType.REGULAR((3,)),
            dma((6,)), dma((2, 2, 4)), dma((2, 2, 4)), dma((2, 2, 3)), dma((2, 2, 3)),
            dma((16,)), dma((16,)), dma((2,)), dma((2,)), dma((2, zs)), dma((2, zs)), dma((8,)), dma((8,)), dma((16,)), dma((16,)),
        ],
        compiler_params=pltpu.CompilerParams(collective_id=0, has_side_effects=True, vmem_limit_bytes=32 << 20),
    )(
        *(
            pltpu.with_memory_space_constraint(a, pltpu.HBM)
            for a in (
                gate_grads, gate_rows.reshape(1, 128), gate_cols.reshape(32, 128),
                out_grads, out_rows.reshape(4, 128), out_cols.reshape(8, 128),
            )
        )
    )
    outs = pl.pallas_call(
        finish,
        out_shape=(
            jax.ShapeDtypeStruct((128, 4096), BF16),
            jax.ShapeDtypeStruct((1, 128), F32),
            jax.ShapeDtypeStruct((32, 128), F32),
            jax.ShapeDtypeStruct((512, 1024), BF16),
            jax.ShapeDtypeStruct((4, 128), F32),
            jax.ShapeDtypeStruct((8, 128), F32),
        ),
        in_specs=[vmem] * 9,
        out_specs=(hbm,) * 6,
        scratch_shapes=[buf((128, 4096), BF16), buf((512, 1024), BF16), dma((12,))],
        compiler_params=pltpu.CompilerParams(vmem_limit_bytes=32 << 20),
    )(*held)
    gate_up, gate_r, gate_c, out_up, out_r, out_c = outs
    return gate_up, gate_r.reshape(128), gate_c.reshape(4096), out_up, out_r.reshape(512), out_c.reshape(1024)


def solution(mesh):
    in_specs = (P("dp", "row", "col"), P("row"), P("col"), P("dp", "row", "col"), P("row"), P("col"))
    out_specs = (P("row", "col"), P("row"), P("col"), P("row", "col"), P("row"), P("col"))
    return jax.shard_map(
        functools.partial(local, mesh.shape["row"] // 2), mesh=mesh, in_specs=in_specs, out_specs=out_specs, check_vma=False
    )
```
